128 devices in a mesh: seq: 32 (over z, x, core), head: 4 (over y).
Axes of the slice: x: 4, y: 4, z: 4, core: 2. Of those that a mesh axis runs over, the one named last changes fastest.
Arguments:
- queries: bfloat16 [65536, 2048], P('seq', 'head'), may hold values from -8 to 8
- key_rows: bfloat16 [65536, 2048], P('seq', 'head'), may hold values from -8 to 8
- value_rows: bfloat16 [65536, 2048], P('seq', 'head'), may hold values from -6 to 6
- cluster_ids: int32 [16, 65536, 1], P('head', 'seq'), may hold values from 0 to 255; in each aligned block of 2048 rows (0 to 2047, 2048 to 4095, ..., all dimensions but the last counted through in order) at most 12 rows name the same one
- centroids: float32 [16, 256, 128], P('head', 'seq'), may hold values from -6 to 6
- out_weight: bfloat16 [2048, 2048], P('head'), may hold values from -0.125 to 0.125
Outputs:
- mixed: bfloat16 [65536, 2048], P(('seq', 'head'))
- new_centroids: float32 [16, 256, 128], P('head', 'seq')
The draws below stay inside these ranges and needn't reach their ends.
Inputs may be any that keep to these rules, and one draw needn't show every extreme that they name: `cluster_ids`: in each head and among the 2048 tokens of each index of seq, no cluster holds more than 12 tokens, and some cluster holds exactly 12.
All inputs are finite; a program needn't handle non-finite values.
Results may differ from the reference program's by a relative error of at most 0.0056.
Values may be sent and summed in bfloat16 or wider, within the bound.
A program may use at most 128 MiB of HBM per device.

```python
import math
import jax
import jax.numpy as jnp
import numpy as np
from jax import lax

HEADS = 16
HD = 128
CLUSTERS = 256
TOK_DEV = 2048
CAP = 12
TOKENS = 65536
D = 2048
PRIOR = 8
N_SEQ = 32


def rising_scale(lowest, highest):
    position = jnp.arange(TOKENS, dtype=jnp.float32) / TOKENS
    return jnp.exp(math.log(lowest) + position * math.log(highest / lowest))[:, None, None]


def draw_queries(key, part):
    key = jax.random.fold_in(key, 1)
    drawn = jax.random.normal(key, (TOKENS, HEADS * HD), jnp.float32)
    return jnp.clip(drawn, -8.0, 8.0).astype(jnp.bfloat16)


def draw_key_rows(key, part):
    key = jax.random.fold_in(key, 2)
    ramp = rising_scale(0.6, 2.4)
    drawn = (ramp * jax.random.normal(key, (TOKENS, HEADS, HD), jnp.float32)).reshape(TOKENS, HEADS * HD)
    return jnp.clip(drawn, -8.0, 8.0).astype(jnp.bfloat16)


def block_levels(stream_key, extent, shards, low, high):
    gain = 1.0
    for dim, shards_of in shards:
        steps = jax.random.uniform(jax.random.fold_in(jax.random.fold_in(stream_key, 6), dim), (shards_of,), jnp.float32, low / len(shards), high / len(shards))
        gain = gain * jnp.repeat(jnp.exp(steps), extent[dim] // shards_of).reshape((-1,) + (1,) * (len(extent) - 1 - dim))
    return gain


def assign_block(stream_key, own, number, rows, amount, top, most, skew):
    sequence = jax.random.permutation(stream_key, amount)
    packed, common = shares(amount, rows * top, most, skew, True), shares(amount, rows * top, most, skew, False)
    places = jnp.arange(amount)

    def named(lengths, offset_by):
        used = int((lengths > 0).sum())
        fixed = max(1, used // 4)
        shifted = fixed + (places - fixed + offset_by * (used - fixed)) % max(1, amount - fixed)
        return jnp.zeros((amount,), jnp.int32).at[sequence[jnp.where(places < fixed, places, shifted)]].set(jnp.asarray(lengths, jnp.int32))

    lengths = jnp.where(number % 4 == 0, named(packed, number // 4), named(common, number - number // 4 - 1))
    mixed = jax.random.permutation(jax.random.fold_in(own, 3), amount)
    source_of, receiver = mixed[0:amount // 2 * 2:2], mixed[1:amount // 2 * 2:2]
    margin = jnp.minimum(lengths[source_of] - 1, most - lengths[receiver]) // 2
    margin = jnp.where((source_of == sequence[0]) | (receiver == sequence[0]) | (lengths[receiver] == 0), 0, jnp.maximum(margin, 0))
    shifted = jax.random.randint(jax.random.fold_in(own, 4), (amount // 2,), 0, 1 << 20) % (margin + 1)
    lengths = lengths.at[source_of].add(-shifted).at[receiver].add(shifted)
    labels = jnp.searchsorted(jnp.cumsum(lengths), jnp.arange(rows * top), side="right").astype(jnp.int32)
    listing = labels.reshape(top, rows).T
    listing = listing[jax.random.permutation(jax.random.fold_in(own, 1), rows)]
    offset_by = jax.random.randint(jax.random.fold_in(own, 2), (rows, 1), 0, top)
    return jnp.take_along_axis(listing, (jnp.arange(top)[None, :] + offset_by) % top, axis=1)


def shares(amount, total, limit, lean, full):
    loads = [(1 << 20) // math.isqrt(rank ** lean) + 1 for rank in range(1, amount + 1)]
    largest = limit if full else min(limit, max(-(-total // amount), total * loads[0] // sum(loads)))
    least = 1 if total - largest >= amount - 1 else 0
    holding, surplus = [largest] + [least] * (amount - 1), total - largest - least * (amount - 1)
    while surplus > 0:
        movable = [i for i in range(1, amount) if holding[i] < largest] or [i for i in range(1, amount) if holding[i] < limit]
        whole, left = sum([loads[i] for i in movable]), surplus
        for i in movable:
            more = min(limit - holding[i], max(1, left * loads[i] // whole), surplus)
            holding[i] = holding[i] + more
            surplus = surplus - more
    return np.array(holding)


def gaussian(rng, extent, deviation, limit, pieces=(), held_as=jnp.bfloat16):
    entries = deviation * jax.random.normal(rng, extent, jnp.float32)
    if pieces:
        entries = entries * block_levels(rng, extent, pieces, -0.22, 0.18)
    return jnp.clip(entries, -limit, limit).astype(held_as)


def setup_inputs(seed: int = 0) -> dict:
    streams_of = jax.random.split(jax.random.key(seed), 7)
    queries = draw_queries(jax.random.fold_in(streams_of[6], 71), 0)
    key_rows = draw_key_rows(jax.random.fold_in(streams_of[6], 71), 0)
    value_rows = gaussian(streams_of[2], (TOKENS, D), 1.0, 6.0, ((0, 32), (1, 4)))
    cluster_ids_keys = jax.random.split(jax.random.fold_in(streams_of[3], 1), HEADS * TOKENS // TOK_DEV)
    cluster_ids_turns = jax.random.permutation(jax.random.fold_in(streams_of[3], 3), HEADS * TOKENS // TOK_DEV)
    cluster_ids = jax.vmap(lambda own, number: assign_block(jax.random.fold_in(streams_of[3], 2), own, number, TOK_DEV, CLUSTERS, 1, CAP, 2))(cluster_ids_keys, cluster_ids_turns).reshape((HEADS, TOKENS, 1))
    centroids = gaussian(streams_of[4], (HEADS, CLUSTERS, HD), 1.0, 6.0, ((0, 4), (1, 32)), jnp.float32)
    out_weight = gaussian(streams_of[5], (D, D), D ** -0.5, 0.125, ((0, 4),))
    return dict(queries=queries, key_rows=key_rows, value_rows=value_rows, cluster_ids=cluster_ids, centroids=centroids, out_weight=out_weight)


def split_heads(matrix):
    return jnp.transpose(matrix.reshape(TOKENS, HEADS, HD), (1, 0, 2))

def reference(queries, key_rows, value_rows, cluster_ids, centroids, out_weight):
    member_rows = N_SEQ * CAP
    score_scale = 1.0 / math.sqrt(HD)
    query_heads = split_heads(queries)
    key_heads = split_heads(key_rows)
    value_heads = split_heads(value_rows)
    head_ids = cluster_ids[:, :, 0]

    def one_head(inputs):
        query_one, key_one, value_one, assigned = inputs
        padding = jnp.zeros((1, HD), jnp.bfloat16)
        query_pad = jnp.concatenate([query_one, padding], axis=0)
        key_pad = jnp.concatenate([key_one, padding], axis=0)
        value_pad = jnp.concatenate([value_one, padding], axis=0)

        def one_cluster(cluster):
            members = jnp.nonzero(assigned == cluster, size=member_rows, fill_value=TOKENS)[0].astype(jnp.int32)
            query_part = query_pad[members]
            key_part = key_pad[members]
            value_part = value_pad[members]
            scores = jnp.dot(query_part, key_part.T, preferred_element_type=jnp.float32) * score_scale
            allowed = (members[None, :] < TOKENS) & (members[None, :] <= members[:, None])
            scores = jnp.where(allowed, scores, -1e+30)
            row_max = lax.optimization_barrier(jnp.max(scores, axis=-1, keepdims=True))
            raw_weights = jnp.exp(scores - row_max)
            weights = (raw_weights / lax.optimization_barrier(jnp.sum(raw_weights, axis=-1, keepdims=True))).astype(jnp.bfloat16)
            result = jnp.dot(weights, value_part, preferred_element_type=jnp.float32).astype(jnp.bfloat16)
            return (members, result)
        all_members, all_results = lax.map(one_cluster, jnp.arange(CLUSTERS, dtype=jnp.int32))
        merged = jnp.zeros((TOKENS + 1, HD), jnp.bfloat16)
        merged = merged.at[all_members.reshape(-1)].set(all_results.reshape(-1, HD))
        return merged[:TOKENS]
    head_results = lax.map(one_head, (query_heads, key_heads, value_heads, head_ids))
    attended = jnp.transpose(head_results, (1, 0, 2)).reshape(TOKENS, D)
    mixed = jnp.dot(attended, out_weight, preferred_element_type=jnp.float32).astype(jnp.bfloat16)

    def head_sums(inputs):
        key_one, assigned = inputs
        sums = jax.ops.segment_sum(key_one.astype(jnp.float32), assigned, num_segments=CLUSTERS)
        counts = jax.ops.segment_sum(jnp.ones((TOKENS,), jnp.float32), assigned, num_segments=CLUSTERS)
        return (sums, counts)
    key_sums, key_counts = lax.map(head_sums, (key_heads, head_ids))
    new_centroids = (PRIOR * centroids + key_sums) / (PRIOR + key_counts)[..., None]
    return (mixed, new_centroids)
```

```python
import functools
import math

import jax
import jax.numpy as jnp
import numpy as np
from jax import lax
from jax.experimental import pallas as pl
from jax.experimental.pallas import tpu as pltpu
from jax.sharding import PartitionSpec as P

HD = 128
CLUSTERS = 256
CAP = 12
PRIOR = 8.0
N_SEQ = 32
N_HEAD = 4
OWN = CLUSTERS // N_SEQ
CHUNK = OWN * CAP
TOK = 2048
HEADS = 4
GROUP = 4
ROWS = GROUP * CHUNK
MEMBERS = N_SEQ * CAP
BLOCK = 128
TBLOCK = TOK // N_HEAD
MARK = 64.0
NEG = -1e30
MESH = pl.DeviceIdType.MESH
BF = jnp.bfloat16
F32 = jnp.float32
ORDER = (0, 1, 2, 6, 3, 7, 8, 24, 9, 25, 4, 5, 10, 30, 11, 31, 14, 26, 15, 27, 16, 17, 12, 28, 13, 29, 18, 22, 19, 23, 20, 21)


def rearrangement():
    src, clu, rank = np.meshgrid(np.arange(GROUP), np.arange(OWN), np.arange(CAP), indexing="ij")
    matrix = np.zeros((ROWS, ROWS), np.float32)
    matrix[(clu * GROUP * CAP + src * CAP + rank).ravel(), (src * CHUNK + clu * CAP + rank).ravel()] = 1
    return matrix


def kernel(
    q_ref, k_ref, v_ref, ids_ref, cent_ref, w_ref, perm_ref, back_ref,
    out_ref, nc_ref,
    x_ref, base_ref, p_ref, send, recv, aq, ak, av, oarr, rsend, rrecv, lo_ref, pt_ref, atok, ytok, wall, acc,
    xsem, qs, qr, rs, rr, ys, yr, ws, wr, wl,
):
    me = lax.axis_index("seq")
    hh = lax.axis_index("head")
    z, x, core = me // 8, (me // 2) % 4, me % 2

    def peer(k):
        dz, dx, dc = k // 8, (k // 2) % 4, k % 2
        a = dz + core * (dx - dz)
        b = dx + core * (dz - dx)
        return ((z + a) % 4) * 8 + ((x + b) % 4) * 2 + (core + dc) % 2

    def loads(h, slot):
        cols = pl.ds(pl.multiple_of(h * HD, HD), HD)
        return [
            pltpu.make_async_copy(ref.at[:, cols], x_ref.at[slot, :, pl.ds(i * HD, HD)], xsem.at[slot, i])
            for i, ref in enumerate((q_ref, k_ref, v_ref))
        ]

    barrier = pltpu.get_barrier_semaphore()

    @pl.loop(1, N_SEQ)
    def _(k):
        pl.semaphore_signal(barrier, inc=1, device_id=(peer(k), hh), device_id_type=MESH)

    @pl.loop(1, N_HEAD)
    def _(k):
        pl.semaphore_signal(barrier, inc=1, device_id=(me, (hh + k) % N_HEAD), device_id_type=MESH)

    for slot in range(2):
        for copy in loads(slot, slot):
            copy.start()
    own_weight = pltpu.make_async_copy(w_ref, wall.at[:, hh], wl)
    own_weight.start()

    lane0 = lax.broadcasted_iota(jnp.int32, (TOK, HD), 1) == 0
    x_ref[0, :, 3 * HD :] = jnp.where(lane0, MARK, 0.0).astype(BF)
    x_ref[1, :, 3 * HD :] = jnp.where(lane0, MARK, 0.0).astype(BF)
    first = (lax.broadcasted_iota(jnp.int32, (16, HD), 0) == 0) & (lax.broadcasted_iota(jnp.int32, (16, HD), 1) == 0)
    for c in range(OWN):
        aq[c, MEMBERS : MEMBERS + 16, :] = jnp.where(first, 1.0, 0.0).astype(BF)

    pl.semaphore_wait(barrier, N_SEQ - 1 + N_HEAD - 1)

    @pl.loop(1, N_HEAD)
    def _(k):
        pltpu.make_async_remote_copy(
            w_ref, wall.at[:, hh], ws, wr, device_id=(me, (hh + k) % N_HEAD), device_id_type=MESH
        ).start()

    @pl.loop(0, HEADS)
    def _(h):
        slot = h % 2
        before = jnp.where(
            lax.broadcasted_iota(jnp.int32, (256, 256), 0) < lax.broadcasted_iota(jnp.int32, (256, 256), 1), 1.0, 0.0
        ).astype(BF)
        cluster = lax.broadcasted_iota(jnp.int32, (CLUSTERS, 256), 0)
        sofar = jnp.zeros((CLUSTERS, 1), F32)
        row96 = lax.broadcasted_iota(jnp.int32, (CHUNK, 256), 0)
        lane = lax.broadcasted_iota(jnp.int32, (256, 128), 1)
        for b in range(TOK // 256):
            cols = slice(256 * b, 256 * b + 256)
            named = ids_ref[pl.ds(h, 1), cols]
            hot = jnp.where(cluster == named, 1.0, 0.0)
            earlier = jnp.dot(hot.astype(BF), before, preferred_element_type=F32)
            rank = jnp.sum(hot * (earlier + sofar), axis=0, keepdims=True).astype(jnp.int32)
            sofar = sofar + jnp.sum(hot, axis=1, keepdims=True)
            within = (named & 7) * CAP + rank
            owner = (named >> 3).astype(F32)
            base_ref[:, cols] = jnp.where(row96 == within, owner, -1.0).astype(BF)
            place = jnp.broadcast_to((named * CAP + rank).astype(F32), (128, 256)).T.astype(jnp.int32)
            lo_ref[h, cols, :] = jnp.where((place & 127) == lane, (place >> 7).astype(F32), -1.0).astype(BF)
        for copy in loads(h, slot):
            copy.wait()
        mark = jnp.where(lax.broadcasted_iota(jnp.int32, (ROWS, HD), 1) == 0, MARK, 0.0)
        for j in range(N_SEQ // GROUP):
            targets = [peer(k) for k in ORDER[GROUP * j : GROUP * j + GROUP]]
            for i, target in enumerate(targets):
                p_ref[CHUNK * i : CHUNK * i + CHUNK, :] = jnp.where(
                    base_ref[...] == target.astype(F32).astype(BF), 1.0, 0.0
                ).astype(BF)
            rows = jnp.dot(p_ref[...], x_ref[slot], preferred_element_type=F32)
            keys = rows[:, HD : 2 * HD] + (mark - rows[:, 3 * HD :])
            rows = jnp.concatenate([rows[:, :HD], keys, rows[:, 2 * HD : 3 * HD]], axis=1).astype(BF)
            rows = rows.reshape(GROUP, CHUNK, 3 * HD)
            send[h, GROUP * j : GROUP * j + GROUP] = rows
            for i, target in enumerate(targets):
                if GROUP * j + i == 0:
                    recv[h, me] = rows[0]
                else:
                    pltpu.make_async_remote_copy(
                        send.at[h, GROUP * j + i], recv.at[h, me], qs.at[h], qr.at[h],
                        device_id=(target, hh), device_id_type=MESH,
                    ).start()

        @pl.when(h < HEADS - 2)
        def _():
            for copy in loads(h + 2, slot):
                copy.start()

    def arrivals(h):
        others = pl.ds(0, N_SEQ - 1)
        return pltpu.make_async_remote_copy(
            send.at[h, others], recv.at[h, others], qs.at[h], qr.at[h], device_id=(me, hh), device_id_type=MESH
        )

    def returns(h):
        others = pl.ds(0, N_SEQ - 1)
        return pltpu.make_async_remote_copy(
            rsend.at[h, others], rrecv.at[h, others], rs.at[h], rr.at[h], device_id=(me, hh), device_id_type=MESH
        )

    def exchanged(h):
        return pltpu.make_async_remote_copy(
            atok.at[h, pl.ds(0, N_HEAD - 1)], ytok.at[h, :, pl.ds(0, (N_HEAD - 1) * HD)], ys.at[h], yr.at[h],
            device_id=(me, hh), device_id_type=MESH,
        )

    @pl.loop(0, HEADS)
    def _(h):
        arrivals(h).wait_recv()

        @pl.loop(0, N_SEQ // GROUP)
        def _(g):
            piece = recv[h, pl.ds(g * GROUP, GROUP)].reshape(ROWS, 3 * HD)
            moved = jnp.dot(perm_ref[...], piece, preferred_element_type=F32).astype(BF)
            for c in range(OWN):
                part = moved[48 * c : 48 * c + 48]
                where = pl.ds(pl.multiple_of(g * 48, 16), 48)
                aq[c, where, :] = part[:, :HD]
                ak[c, where, :] = part[:, HD : 2 * HD]
                av[c, where, :] = part[:, 2 * HD :]

        factor = math.log2(math.e) / math.sqrt(HD)

        @pl.loop(0, OWN)
        def _(c):
            keys = ak[c]
            values = av[c]
            causal = jnp.where(
                lax.broadcasted_iota(jnp.int32, (BLOCK, BLOCK), 1) <= lax.broadcasted_iota(jnp.int32, (BLOCK, BLOCK), 0),
                0.0, NEG,
            )
            bias = None
            for r in (2, 1, 0):
                width = BLOCK * (r + 1)
                rows = aq[c, BLOCK * r : (MEMBERS + 16 if r == 2 else BLOCK * (r + 1)), :]
                scores = lax.dot_general(
                    rows, keys[:width], (((1,), (1,)), ((), ())), preferred_element_type=F32
                )
                if r == 2:
                    present = jnp.where(scores[BLOCK : BLOCK + 1, :] < MARK / 2, 1.0, 0.0)
                    bias = jnp.where(present > 0.5, 0.0, NEG)
                    present8 = jnp.broadcast_to(present, (8, MEMBERS))
                    sums = jnp.dot(present8.astype(BF), keys, preferred_element_type=F32)[0:1]
                    count = jnp.sum(present, axis=1, keepdims=True)
                    nc_ref[h, pl.ds(c, 1), :] = (PRIOR * cent_ref[h, pl.ds(c, 1), :] + sums) / (PRIOR + count)
                    scores = scores[:BLOCK]
                scores = scores * factor + bias[:, :width]
                last = scores[:, width - BLOCK :] + causal
                scores = last if r == 0 else jnp.concatenate([scores[:, : width - BLOCK], last], axis=1)
                top = jnp.max(scores, axis=1, keepdims=True)
                raw = jnp.exp2(scores - top)
                weights = (raw / jnp.sum(raw, axis=1, keepdims=True)).astype(BF)
                oarr[c, BLOCK * r : BLOCK * r + BLOCK, :] = jnp.dot(
                    weights, values[:width], preferred_element_type=F32
                ).astype(BF)

        @pl.loop(0, N_SEQ // GROUP)
        def _(g):
            piece = oarr[:, pl.ds(pl.multiple_of(g * 48, 16), 48), :].reshape(ROWS, HD)
            moved = jnp.dot(back_ref[...], piece, preferred_element_type=F32).astype(BF)
            rsend[h, pl.ds(g * GROUP, GROUP)] = moved.reshape(GROUP, CHUNK, HD)

        rrecv[h, me] = rsend[h, me]
        for k in ORDER[1:]:
            target = peer(k)
            pltpu.make_async_remote_copy(
                rsend.at[h, target], rrecv.at[h, me], rs.at[h], rr.at[h],
                device_id=(target, hh), device_id_type=MESH,
            ).start()

    own_weight.wait()
    pltpu.make_async_remote_copy(
        wall.at[:, pl.ds(0, N_HEAD - 1)], wall.at[:, pl.ds(0, N_HEAD - 1)], ws, wr,
        device_id=(me, hh), device_id_type=MESH,
    ).wait_recv()

    def project(h):
        exchanged(h).wait_recv()
        for n in range(4):
            cols = slice(512 * n, 512 * n + 512)
            part = jnp.dot(
                ytok[h], wall[h, :, :, cols].reshape(N_HEAD * HD, 512), preferred_element_type=F32
            )
            acc[:, cols] = acc[:, cols] + part

    acc[...] = jnp.zeros_like(acc)

    @pl.loop(0, HEADS)
    def _(h):
        returns(h).wait_recv()

        @pl.loop(1, N_HEAD + 1)
        def _(k):
            to = (hh + k) % N_HEAD
            known = lo_ref[h, pl.ds(pl.multiple_of(to * TBLOCK, TBLOCK), TBLOCK), :]
            for j in range(CLUSTERS * CAP // 128):
                pt_ref[:, 128 * j : 128 * j + 128] = jnp.where(known == float(j), 1.0, 0.0).astype(BF)
            rows = jnp.dot(
                pt_ref[...], rrecv[h].reshape(CLUSTERS * CAP, HD), preferred_element_type=F32
            ).astype(BF)
            atok[h, to] = rows

            @pl.when(k < N_HEAD)
            def _():
                pltpu.make_async_remote_copy(
                    atok.at[h, to], ytok.at[h, :, pl.ds(pl.multiple_of(hh * HD, HD), HD)], ys.at[h], yr.at[h],
                    device_id=(me, to), device_id_type=MESH,
                ).start()

        ytok[h, :, pl.ds(pl.multiple_of(hh * HD, HD), HD)] = atok[h, hh]

        @pl.when(h > 0)
        def _():
            project(h - 1)

    project(HEADS - 1)
    out_ref[...] = acc[...].astype(BF)

    @pl.loop(0, HEADS)
    def _(h):
        arrivals(h).wait_send()
        returns(h).wait_send()
        exchanged(h).wait_send()

    pltpu.make_async_remote_copy(
        wall.at[:, pl.ds(0, N_HEAD - 1)], wall.at[:, pl.ds(0, N_HEAD - 1)], ws, wr,
        device_id=(me, hh), device_id_type=MESH,
    ).wait_send()


def shards(queries, key_rows, value_rows, cluster_ids, centroids, out_weight):
    perm = rearrangement()
    hbm = pl.BlockSpec(memory_space=pl.ANY)
    vmem = pl.BlockSpec(memory_space=pltpu.VMEM)
    return pl.pallas_call(
        kernel,
        out_shape=(
            jax.ShapeDtypeStruct((TBLOCK, 2048), BF),
            jax.ShapeDtypeStruct((HEADS, OWN, HD), F32),
        ),
        in_specs=[hbm, hbm, hbm, vmem, vmem, hbm, vmem, vmem],
        out_specs=(vmem, vmem),
        scratch_shapes=[
            pltpu.VMEM((2, TOK, 4 * HD), BF),
            pltpu.VMEM((CHUNK, TOK), BF),
            pltpu.VMEM((ROWS, TOK), BF),
            pltpu.VMEM((HEADS, N_SEQ, CHUNK, 3 * HD), BF),
            pltpu.VMEM((HEADS, N_SEQ, CHUNK, 3 * HD), BF),
            pltpu.VMEM((OWN, MEMBERS + 16, HD), BF),
            pltpu.VMEM((OWN, MEMBERS, HD), BF),
            pltpu.VMEM((OWN, MEMBERS, HD), BF),
            pltpu.VMEM((OWN, MEMBERS, HD), BF),
            pltpu.VMEM((HEADS, N_SEQ, CHUNK, HD), BF),
            pltpu.VMEM((HEADS, N_SEQ, CHUNK, HD), BF),
            pltpu.VMEM((HEADS, TOK, HD), BF),
            pltpu.VMEM((TBLOCK, CLUSTERS * CAP), BF),
            pltpu.VMEM((HEADS, N_HEAD, TBLOCK, HD), BF),
            pltpu.VMEM((HEADS, TBLOCK, N_HEAD * HD), BF),
            pltpu.VMEM((HEADS, N_HEAD, HD, 2048), BF),
            pltpu.VMEM((TBLOCK, 2048), F32),
            pltpu.SemaphoreType.DMA((2, 3)),
            pltpu.SemaphoreType.DMA((HEADS,)),
            pltpu.SemaphoreType.DMA((HEADS,)),
            pltpu.SemaphoreType.DMA((HEADS,)),
            pltpu.SemaphoreType.DMA((HEADS,)),
            pltpu.SemaphoreType.DMA((HEADS,)),
            pltpu.SemaphoreType.DMA((HEADS,)),
            pltpu.SemaphoreType.DMA,
            pltpu.SemaphoreType.DMA,
            pltpu.SemaphoreType.DMA,
        ],
        compiler_params=pltpu.CompilerParams(
            collective_id=0, has_side_effects=True, vmem_limit_bytes=63 << 20
        ),
    )(
        queries, key_rows, value_rows, cluster_ids.reshape(HEADS, TOK), centroids,
        out_weight.reshape(HEADS, HD, 2048),
        jnp.asarray(perm, BF), jnp.asarray(perm.T, BF),
    )


def solution(mesh):
    placed = (
        P("seq", "head"),
        P("seq", "head"),
        P("seq", "head"),
        P("head", "seq", None),
        P("head", "seq", None),
        P("head", None),
    )
    return jax.shard_map(
        shards,
        mesh=mesh,
        in_specs=placed,
        out_specs=(P(("seq", "head"), None), P("head", "seq", None)),
        check_vma=False,
    )
```

```python
import functools
import math

import jax
import jax.numpy as jnp
import numpy as np
from jax import lax
from jax.experimental import pallas as pl
from jax.experimental.pallas import tpu as pltpu
from jax.sharding import PartitionSpec as P

HD = 128
CLUSTERS = 256
CAP = 12
PRIOR = 8.0
N_SEQ = 32
N_HEAD = 4
OWN = CLUSTERS // N_SEQ
CHUNK = OWN * CAP
TOK = 2048
HEADS = 4
GROUP = 4
ROWS = GROUP * CHUNK
MEMBERS = N_SEQ * CAP
BLOCK = 128
TBLOCK = TOK // N_HEAD
MARK = 64.0
NEG = -1e30
MESH = pl.DeviceIdType.MESH
BF = jnp.bfloat16
F32 = jnp.float32
ORDER = (0, 1, 2, 6, 3, 7, 8, 24, 9, 25, 4, 5, 10, 30, 11, 31, 14, 26, 15, 27, 16, 17, 12, 28, 13, 29, 18, 22, 19, 23, 20, 21)
TABLE = tuple(
    (
        sum(k // 8 * 4**n for n, k in enumerate(ORDER[place::4])),
        sum(k % 8 * 8**n for n, k in enumerate(ORDER[place::4])),
    )
    for place in range(4)
)


def rearrangement():
    src, clu, rank = np.meshgrid(np.arange(GROUP), np.arange(OWN), np.arange(CAP), indexing="ij")
    matrix = np.zeros((ROWS, ROWS), np.float32)
    matrix[(clu * GROUP * CAP + src * CAP + rank).ravel(), (src * CHUNK + clu * CAP + rank).ravel()] = 1
    return matrix


def kernel(
    q_ref, k_ref, v_ref, ids_ref, cent_ref, w_ref, perm_ref, back_ref,
    acc_out, y_last, w_last, nc_ref,
    x_ref, base_ref, p_ref, pt_ref, send, recv, aq, ak, av, oarr, rsend, rrecv, lo_ref, atok, ytok, wall, acc,
    xsem, qs, qr, rs, rr, ys, yr, ws, wr, wl, os,
):
    me = lax.axis_index("seq")
    hh = lax.axis_index("head")
    z, x, core = me // 8, (me // 2) % 4, me % 2

    def device_at(dz, dx, dc):
        a = dz + core * (dx - dz)
        b = dx + core * (dz - dx)
        return ((z + a) % 4) * 8 + ((x + b) % 4) * 2 + (core + dc) % 2

    def peer(k):
        return device_at(k // 8, (k // 2) % 4, k % 2)

    def four(table):
        return [device_at(far % 4, (near // 2) % 4, near % 2) for far, near in table]

    def shifted(table):
        return tuple((far // 4, near // 8) for far, near in table)

    def tables():
        return tuple((jnp.int32(far), jnp.int32(near)) for far, near in TABLE)

    def loads(h, slot):
        cols = pl.ds(pl.multiple_of(h * HD, HD), HD)
        return [
            pltpu.make_async_copy(ref.at[:, cols], x_ref.at[slot, :, pl.ds(i * HD, HD)], xsem.at[slot, i])
            for i, ref in enumerate((q_ref, k_ref, v_ref))
        ]

    barrier = pltpu.get_barrier_semaphore()

    @pl.loop(1, N_SEQ)
    def _(k):
        pl.semaphore_signal(barrier, inc=1, device_id=(peer(k), hh), device_id_type=MESH)

    @pl.loop(1, N_HEAD)
    def _(k):
        pl.semaphore_signal(barrier, inc=1, device_id=(me, (hh + k) % N_HEAD), device_id_type=MESH)

    for slot in range(2):
        for copy in loads(slot, slot):
            copy.start()
    own_weight = pltpu.make_async_copy(w_ref, wall.at[:, hh], wl)
    own_weight.start()

    lane0 = lax.broadcasted_iota(jnp.int32, (TOK, HD), 1) == 0
    x_ref[0, :, 3 * HD :] = jnp.where(lane0, MARK, 0.0).astype(BF)
    x_ref[1, :, 3 * HD :] = jnp.where(lane0, MARK, 0.0).astype(BF)
    first = (lax.broadcasted_iota(jnp.int32, (16, HD), 0) == 0) & (lax.broadcasted_iota(jnp.int32, (16, HD), 1) == 0)
    for c in range(OWN):
        aq[c, MEMBERS : MEMBERS + 16, :] = jnp.where(first, 1.0, 0.0).astype(BF)

    @pl.loop(0, HEADS)
    def _(h):
        slot = h % 2
        before = jnp.where(
            lax.broadcasted_iota(jnp.int32, (256, 256), 0) < lax.broadcasted_iota(jnp.int32, (256, 256), 1), 1.0, 0.0
        ).astype(BF)
        cluster = lax.broadcasted_iota(jnp.int32, (CLUSTERS, 256), 0)
        sofar = jnp.zeros((CLUSTERS, 1), F32)
        row96 = lax.broadcasted_iota(jnp.int32, (CHUNK, 256), 0)
        lane = lax.broadcasted_iota(jnp.int32, (256, 128), 1)
        named16 = ids_ref[pl.ds(pl.multiple_of(h * 16, 16), 16), :]
        for b in range(TOK // 256):
            cols = slice(256 * b, 256 * b + 256)
            named = jnp.concatenate([named16[2 * b : 2 * b + 1], named16[2 * b + 1 : 2 * b + 2]], axis=1)
            hot = jnp.where(cluster == named, 1.0, 0.0)
            earlier = jnp.dot(hot.astype(BF), before, preferred_element_type=F32)
            rank = jnp.sum(hot * (earlier + sofar), axis=0, keepdims=True).astype(jnp.int32)
            sofar = sofar + jnp.sum(hot, axis=1, keepdims=True)
            within = (named & 7) * CAP + rank
            owner = (named >> 3).astype(F32)
            base_ref[:, cols] = jnp.where(row96 == within, owner, -1.0).astype(BF)
            place = jnp.broadcast_to((named * CAP + rank).astype(F32), (128, 256)).T.astype(jnp.int32)
            lo_ref[h, cols, :] = jnp.where((place & 127) == lane, (place >> 7).astype(F32), -1.0).astype(BF)
        mark = jnp.where(lax.broadcasted_iota(jnp.int32, (ROWS, HD), 1) == 0, MARK, 0.0)

        for copy in loads(h, slot):
            copy.wait()

        def pack(j, table):
            targets = four(table)
            for i, target in enumerate(targets):
                p_ref[CHUNK * i : CHUNK * i + CHUNK, :] = jnp.where(
                    base_ref[...] == target.astype(F32).astype(BF), 1.0, 0.0
                ).astype(BF)
            rows = jnp.dot(p_ref[...], x_ref[slot], preferred_element_type=F32)
            keys = rows[:, HD : 2 * HD] + (mark - rows[:, 3 * HD :])
            rows = jnp.concatenate([rows[:, :HD], keys, rows[:, 2 * HD : 3 * HD]], axis=1).astype(BF)
            rows = rows.reshape(GROUP, CHUNK, 3 * HD)
            send[h, pl.ds(GROUP * j, GROUP)] = rows

            @pl.when(j == 0)
            def _():
                recv[h, me] = rows[0]

            @pl.when((h == 0) & (j == 0))
            def _():
                pl.semaphore_wait(barrier, N_SEQ - 1 + N_HEAD - 1)

            def ship(i):
                pltpu.make_async_remote_copy(
                    send.at[h, GROUP * j + i], recv.at[h, me], qs.at[h], qr.at[h],
                    device_id=(targets[i], hh), device_id_type=MESH,
                ).start()

            pl.when(j > 0)(functools.partial(ship, 0))
            for i in range(1, GROUP):
                ship(i)

            @pl.when((h == 0) & (j == 0))
            def _():
                @pl.loop(1, N_HEAD)
                def _(k):
                    pltpu.make_async_remote_copy(
                        w_ref, wall.at[:, hh], ws, wr, device_id=(me, (hh + k) % N_HEAD), device_id_type=MESH
                    ).start()

            return shifted(table)

        lax.fori_loop(0, N_SEQ // GROUP, pack, tables())

        @pl.when(h < HEADS - 2)
        def _():
            for copy in loads(h + 2, slot):
                copy.start()

    def arrivals(h):
        others = pl.ds(0, N_SEQ - 1)
        return pltpu.make_async_remote_copy(
            send.at[h, others], recv.at[h, others], qs.at[h], qr.at[h], device_id=(me, hh), device_id_type=MESH
        )

    def returns(h):
        others = pl.ds(0, N_SEQ - 1)
        return pltpu.make_async_remote_copy(
            rsend.at[h, others], rrecv.at[h, others], rs.at[h], rr.at[h], device_id=(me, hh), device_id_type=MESH
        )

    def landing(h, where):
        return y_last.at[:, where] if isinstance(h, int) else ytok.at[h, :, where]

    def exchanged(h):
        return pltpu.make_async_remote_copy(
            atok.at[h, pl.ds(0, N_HEAD - 1)], landing(h, pl.ds(0, (N_HEAD - 1) * HD)), ys.at[h], yr.at[h],
            device_id=(me, hh), device_id_type=MESH,
        )

    @pl.loop(0, HEADS)
    def _(h):
        arrivals(h).wait_recv()

        @pl.loop(0, N_SEQ // GROUP)
        def _(g):
            piece = recv[h, pl.ds(g * GROUP, GROUP)].reshape(ROWS, 3 * HD)
            moved = jnp.dot(perm_ref[...], piece, preferred_element_type=F32).astype(BF)
            for c in range(OWN):
                part = moved[48 * c : 48 * c + 48]
                where = pl.ds(pl.multiple_of(g * 48, 16), 48)
                aq[c, where, :] = part[:, :HD]
                ak[c, where, :] = part[:, HD : 2 * HD]
                av[c, where, :] = part[:, 2 * HD :]

        factor = math.log2(math.e) / math.sqrt(HD)

        def attend(c):
            keys = ak[c]
            values = av[c]
            causal = jnp.where(
                lax.broadcasted_iota(jnp.int32, (BLOCK, BLOCK), 1) <= lax.broadcasted_iota(jnp.int32, (BLOCK, BLOCK), 0),
                0.0, NEG,
            )
            bias = None
            for r in (2, 1, 0):
                width = BLOCK * (r + 1)
                rows = aq[c, BLOCK * r : (MEMBERS + 16 if r == 2 else BLOCK * (r + 1)), :]
                scores = lax.dot_general(
                    rows, keys[:width], (((1,), (1,)), ((), ())), preferred_element_type=F32
                )
                if r == 2:
                    present = jnp.where(scores[BLOCK : BLOCK + 1, :] < MARK / 2, 1.0, 0.0)
                    bias = jnp.where(present > 0.5, 0.0, NEG)
                    present8 = jnp.broadcast_to(present, (8, MEMBERS))
                    sums = jnp.dot(present8.astype(BF), keys, preferred_element_type=F32)[0:1]
                    count = jnp.sum(present, axis=1, keepdims=True)
                    nc_ref[h, pl.ds(c, 1), :] = (PRIOR * cent_ref[h, pl.ds(c, 1), :] + sums) / (PRIOR + count)
                    scores = scores[:BLOCK]
                scores = scores * factor + bias[:, :width]
                last = scores[:, width - BLOCK :] + causal
                scores = last if r == 0 else jnp.concatenate([scores[:, : width - BLOCK], last], axis=1)
                top = jnp.max(scores, axis=1, keepdims=True)
                raw = jnp.exp2(scores - top)
                weights = (raw * (1.0 / jnp.sum(raw, axis=1, keepdims=True))).astype(BF)
                oarr[c, BLOCK * r : BLOCK * r + BLOCK, :] = jnp.dot(
                    weights, values[:width], preferred_element_type=F32
                ).astype(BF)

        pl.loop(0, OWN)(attend)

        @pl.loop(0, N_SEQ // GROUP)
        def _(g):
            piece = oarr[:, pl.ds(pl.multiple_of(g * 48, 16), 48), :].reshape(ROWS, HD)
            moved = jnp.dot(back_ref[...], piece, preferred_element_type=F32).astype(BF)
            rsend[h, pl.ds(g * GROUP, GROUP)] = moved.reshape(GROUP, CHUNK, HD)

        rrecv[h, me] = rsend[h, me]

        def give(j, table):
            targets = four(table)

            def ship(i):
                pltpu.make_async_remote_copy(
                    rsend.at[h, targets[i]], rrecv.at[h, me], rs.at[h], rr.at[h],
                    device_id=(targets[i], hh), device_id_type=MESH,
                ).start()

            pl.when(j > 0)(functools.partial(ship, 0))
            for i in range(1, GROUP):
                ship(i)
            return shifted(table)

        lax.fori_loop(0, N_SEQ // GROUP, give, tables())

    own_weight.wait()
    weights_in = pltpu.make_async_remote_copy(
        wall.at[:, pl.ds(0, N_HEAD - 1)], wall.at[:, pl.ds(0, N_HEAD - 1)], ws, wr,
        device_id=(me, hh), device_id_type=MESH,
    )
    weights_in.wait_recv()
    last_weight = pltpu.make_async_copy(wall.at[HEADS - 1], w_last, os.at[0])
    last_weight.start()

    def project(h):
        exchanged(h).wait_recv()
        for n in range(4):
            cols = slice(512 * n, 512 * n + 512)
            part = jnp.dot(
                ytok[h], wall[h, :, :, cols].reshape(N_HEAD * HD, 512), preferred_element_type=F32
            )
            acc[:, cols] = acc[:, cols] + part

    mine = pl.ds(pl.multiple_of(hh * HD, HD), HD)

    def restore(h):
        returns(h).wait_recv()

        @pl.loop(1, N_HEAD + 1)
        def _(k):
            to = (hh + k) % N_HEAD
            known = lo_ref[h, pl.ds(pl.multiple_of(to * TBLOCK, TBLOCK), TBLOCK), :]
            for j in range(CLUSTERS * CAP // 128):
                pt_ref[:, 128 * j : 128 * j + 128] = jnp.where(known == float(j), 1.0, 0.0).astype(BF)
            atok[h, to] = jnp.dot(
                pt_ref[...], rrecv[h].reshape(CLUSTERS * CAP, HD), preferred_element_type=F32
            ).astype(BF)

            @pl.when(k < N_HEAD)
            def _():
                pltpu.make_async_remote_copy(
                    atok.at[h, to], landing(h, mine), ys.at[h], yr.at[h], device_id=(me, to), device_id_type=MESH
                ).start()

    acc[...] = jnp.zeros_like(acc)

    @pl.loop(0, HEADS - 1)
    def _(h):
        restore(h)
        ytok[h, :, mine] = atok[h, hh]

        @pl.when(h > 0)
        def _():
            project(h - 1)

    restore(HEADS - 1)
    own_last = pltpu.make_async_copy(atok.at[HEADS - 1, hh], y_last.at[:, mine], os.at[1])
    own_last.start()

    @pl.loop(HEADS - 2, HEADS - 1)
    def _(h):
        project(h)

    total = pltpu.make_async_copy(acc, acc_out, os.at[2])
    total.start()
    exchanged(HEADS - 1).wait_recv()
    own_last.wait()
    last_weight.wait()
    total.wait()

    @pl.loop(0, HEADS)
    def _(h):
        arrivals(h).wait_send()
        returns(h).wait_send()

    @pl.loop(0, HEADS - 1)
    def _(h):
        exchanged(h).wait_send()

    exchanged(HEADS - 1).wait_send()
    weights_in.wait_send()


def finish(acc_ref, y_ref, w_ref, nc_in, out_ref, nc_out):
    out_ref[...] = (acc_ref[...] + jnp.dot(y_ref[...], w_ref[...], preferred_element_type=F32)).astype(BF)
    nc_out[...] = nc_in[...]


def shards(queries, key_rows, value_rows, cluster_ids, centroids, out_weight):
    perm = rearrangement()
    hbm = pl.BlockSpec(memory_space=pl.ANY)
    vmem = pl.BlockSpec(memory_space=pltpu.VMEM)
    total, y_last, w_last, centers = pl.pallas_call(
        kernel,
        out_shape=(
            jax.ShapeDtypeStruct((TBLOCK, 2048), F32),
            jax.ShapeDtypeStruct((TBLOCK, N_HEAD * HD), BF),
            jax.ShapeDtypeStruct((N_HEAD, HD, 2048), BF),
            jax.ShapeDtypeStruct((HEADS, OWN, HD), F32),
        ),
        in_specs=[hbm, hbm, hbm, vmem, vmem, hbm, vmem, vmem],
        out_specs=(hbm, hbm, hbm, vmem),
        scratch_shapes=[
            pltpu.VMEM((2, TOK, 4 * HD), BF),
            pltpu.VMEM((CHUNK, TOK), BF),
            pltpu.VMEM((ROWS, TOK), BF),
            pltpu.VMEM((TBLOCK, CLUSTERS * CAP), BF),
            pltpu.VMEM((HEADS, N_SEQ, CHUNK, 3 * HD), BF),
            pltpu.VMEM((HEADS, N_SEQ, CHUNK, 3 * HD), BF),
            pltpu.VMEM((OWN, MEMBERS + 16, HD), BF),
            pltpu.VMEM((OWN, MEMBERS, HD), BF),
            pltpu.VMEM((OWN, MEMBERS, HD), BF),
            pltpu.VMEM((OWN, MEMBERS, HD), BF),
            pltpu.VMEM((HEADS, N_SEQ, CHUNK, HD), BF),
            pltpu.VMEM((HEADS, N_SEQ, CHUNK, HD), BF),
            pltpu.VMEM((HEADS, TOK, HD), BF),
            pltpu.VMEM((HEADS, N_HEAD, TBLOCK, HD), BF),
            pltpu.VMEM((HEADS - 1, TBLOCK, N_HEAD * HD), BF),
            pltpu.VMEM((HEADS, N_HEAD, HD, 2048), BF),
            pltpu.VMEM((TBLOCK, 2048), F32),
            pltpu.SemaphoreType.DMA((2, 3)),
            pltpu.SemaphoreType.DMA((HEADS,)),
            pltpu.SemaphoreType.DMA((HEADS,)),
            pltpu.SemaphoreType.DMA((HEADS,)),
            pltpu.SemaphoreType.DMA((HEADS,)),
            pltpu.SemaphoreType.DMA((HEADS,)),
            pltpu.SemaphoreType.DMA((HEADS,)),
            pltpu.SemaphoreType.DMA,
            pltpu.SemaphoreType.DMA,
            pltpu.SemaphoreType.DMA,
            pltpu.SemaphoreType.DMA((3,)),
        ],
        compiler_params=pltpu.CompilerParams(
            collective_id=0, has_side_effects=True, vmem_limit_bytes=63 << 20
        ),
    )(
        queries, key_rows, value_rows, cluster_ids.reshape(HEADS * TOK // 128, 128), centroids,
        out_weight.reshape(HEADS, HD, 2048),
        jnp.asarray(perm, BF), jnp.asarray(perm.T, BF),
    )
    tile = 512
    return pl.pallas_call(
        finish,
        grid=(2048 // tile,),
        out_shape=(
            jax.ShapeDtypeStruct((TBLOCK, 2048), BF),
            jax.ShapeDtypeStruct((HEADS, OWN, HD), F32),
        ),
        in_specs=[
            pl.BlockSpec((TBLOCK, tile), lambda n: (0, n)),
            pl.BlockSpec((TBLOCK, N_HEAD * HD), lambda n: (0, 0)),
            pl.BlockSpec((N_HEAD * HD, tile), lambda n: (0, n)),
            pl.BlockSpec((HEADS, OWN, HD), lambda n: (0, 0, 0)),
        ],
        out_specs=(
            pl.BlockSpec((TBLOCK, tile), lambda n: (0, n)),
            pl.BlockSpec((HEADS, OWN, HD), lambda n: (0, 0, 0)),
        ),
    )(total, y_last, w_last.reshape(N_HEAD * HD, 2048), centers)


def solution(mesh):
    placed = (
        P("seq", "head"),
        P("seq", "head"),
        P("seq", "head"),
        P("head", "seq", None),
        P("head", "seq", None),
        P("head", None),
    )
    return jax.shard_map(
        shards,
        mesh=mesh,
        in_specs=placed,
        out_specs=(P(("seq", "head"), None), P("head", "seq", None)),
        check_vma=False,
    )
```

```python
import functools
import math

import jax
import jax.numpy as jnp
import numpy as np
from jax import lax
from jax.experimental import pallas as pl
from jax.experimental.pallas import tpu as pltpu
from jax.sharding import PartitionSpec as P

HD = 128
CLUSTERS = 256
CAP = 12
PRIOR = 8.0
N_SEQ = 32
N_HEAD = 4
OWN = CLUSTERS // N_SEQ
CHUNK = OWN * CAP
TOK = 2048
HEADS = 4
GROUP = 4
ROWS = GROUP * CHUNK
MEMBERS = N_SEQ * CAP
BLOCK = 128
TBLOCK = TOK // N_HEAD
MARK = 64.0
NEG = -1e30
MESH = pl.DeviceIdType.MESH
BF = jnp.bfloat16
F32 = jnp.float32
ORDER = (0, 1, 2, 6, 3, 7, 8, 24, 9, 25, 4, 5, 10, 30, 11, 31, 14, 26, 15, 27, 16, 17, 12, 28, 13, 29, 18, 22, 19, 23, 20, 21)
TABLE = tuple(
    (
        sum(k // 8 * 4**n for n, k in enumerate(ORDER[place::4])),
        sum(k % 8 * 8**n for n, k in enumerate(ORDER[place::4])),
    )
    for place in range(4)
)


def rearrangement():
    src, clu, rank = np.meshgrid(np.arange(GROUP), np.arange(OWN), np.arange(CAP), indexing="ij")
    matrix = np.zeros((ROWS, ROWS), np.float32)
    matrix[(clu * GROUP * CAP + src * CAP + rank).ravel(), (src * CHUNK + clu * CAP + rank).ravel()] = 1
    return matrix


def one_where(held, wanted):
    apart = held - wanted
    return jnp.maximum(BF(1) - apart * apart, BF(0))


def kernel(
    q_ref, k_ref, v_ref, ids_ref, cent_ref, w_ref, perm_ref, back_ref,
    acc_out, y_last, w_last, nc_ref,
    x_ref, base_ref, p_ref, pt_ref, send, recv, aq, ak, av, oarr, rsend, rrecv, lo_ref, atok, ytok, wall, acc,
    xsem, qs, qr, rs, rr, ys, yr, ws, wr, wl, os,
):
    me = lax.axis_index("seq")
    hh = lax.axis_index("head")
    z, x, core = me // 8, (me // 2) % 4, me % 2

    def device_at(dz, dx, dc):
        a = dz + core * (dx - dz)
        b = dx + core * (dz - dx)
        return ((z + a) % 4) * 8 + ((x + b) % 4) * 2 + (core + dc) % 2

    def peer(k):
        return device_at(k // 8, (k // 2) % 4, k % 2)

    def four(table):
        return [device_at(far % 4, (near // 2) % 4, near % 2) for far, near in table]

    def shifted(table):
        return tuple((far // 4, near // 8) for far, near in table)

    def tables():
        return tuple((jnp.int32(far), jnp.int32(near)) for far, near in TABLE)

    def loads(h, slot):
        cols = pl.ds(pl.multiple_of(h * HD, HD), HD)
        return [
            pltpu.make_async_copy(ref.at[:, cols], x_ref.at[slot, :, pl.ds(i * HD, HD)], xsem.at[slot, i])
            for i, ref in enumerate((q_ref, k_ref, v_ref))
        ]

    barrier = pltpu.get_barrier_semaphore()

    @pl.loop(1, N_SEQ)
    def _(k):
        pl.semaphore_signal(barrier, inc=1, device_id=(peer(k), hh), device_id_type=MESH)

    @pl.loop(1, N_HEAD)
    def _(k):
        pl.semaphore_signal(barrier, inc=1, device_id=(me, (hh + k) % N_HEAD), device_id_type=MESH)

    for slot in range(2):
        for copy in loads(slot, slot):
            copy.start()
    own_weight = pltpu.make_async_copy(w_ref, wall.at[:, hh], wl)
    own_weight.start()

    lane0 = lax.broadcasted_iota(jnp.int32, (TOK, HD), 1) == 0
    x_ref[0, :, 3 * HD :] = jnp.where(lane0, MARK, 0.0).astype(BF)
    x_ref[1, :, 3 * HD :] = jnp.where(lane0, MARK, 0.0).astype(BF)
    first = (lax.broadcasted_iota(jnp.int32, (16, HD), 0) == 0) & (lax.broadcasted_iota(jnp.int32, (16, HD), 1) == 0)
    for c in range(OWN):
        aq[c, MEMBERS : MEMBERS + 16, :] = jnp.where(first, 1.0, 0.0).astype(BF)

    @pl.loop(0, HEADS)
    def _(h):
        slot = h % 2
        before = jnp.where(
            lax.broadcasted_iota(jnp.int32, (256, 256), 0) < lax.broadcasted_iota(jnp.int32, (256, 256), 1), 1.0, 0.0
        ).astype(BF)
        cluster = lax.broadcasted_iota(jnp.int32, (CLUSTERS, 256), 0)
        sofar = jnp.zeros((CLUSTERS, 1), F32)
        row96 = lax.broadcasted_iota(jnp.int32, (CHUNK, 256), 0)
        lane = lax.broadcasted_iota(jnp.int32, (256, 128), 1)
        named16 = ids_ref[pl.ds(pl.multiple_of(h * 16, 16), 16), :]
        for b in range(TOK // 256):
            cols = slice(256 * b, 256 * b + 256)
            named = jnp.concatenate([named16[2 * b : 2 * b + 1], named16[2 * b + 1 : 2 * b + 2]], axis=1)
            hot = jnp.where(cluster == named, 1.0, 0.0)
            earlier = jnp.dot(hot.astype(BF), before, preferred_element_type=F32)
            rank = jnp.sum(hot * (earlier + sofar), axis=0, keepdims=True).astype(jnp.int32)
            sofar = sofar + jnp.sum(hot, axis=1, keepdims=True)
            within = (named & 7) * CAP + rank
            owner = (named >> 3).astype(F32)
            base_ref[:, cols] = jnp.where(row96 == within, owner, -1.0).astype(BF)
            place = jnp.broadcast_to((named * CAP + rank).astype(F32), (128, 256)).T.astype(jnp.int32)
            lo_ref[h, cols, :] = jnp.where((place & 127) == lane, (place >> 7).astype(F32), -1.0).astype(BF)
        mark = jnp.where(lax.broadcasted_iota(jnp.int32, (ROWS, HD), 1) == 0, MARK, 0.0)

        for copy in loads(h, slot):
            copy.wait()

        def pack(j, table):
            targets = four(table)
            for i, target in enumerate(targets):
                p_ref[CHUNK * i : CHUNK * i + CHUNK, :] = one_where(base_ref[...], target.astype(F32).astype(BF))
            rows = jnp.dot(p_ref[...], x_ref[slot], preferred_element_type=F32)
            keys = rows[:, HD : 2 * HD] + (mark - rows[:, 3 * HD :])
            rows = jnp.concatenate([rows[:, :HD], keys, rows[:, 2 * HD : 3 * HD]], axis=1).astype(BF)
            rows = rows.reshape(GROUP, CHUNK, 3 * HD)
            send[h, pl.ds(GROUP * j, GROUP)] = rows

            @pl.when(j == 0)
            def _():
                recv[h, me] = rows[0]

            @pl.when((h == 0) & (j == 0))
            def _():
                pl.semaphore_wait(barrier, N_SEQ - 1 + N_HEAD - 1)

            def ship(i):
                pltpu.make_async_remote_copy(
                    send.at[h, GROUP * j + i], recv.at[h, me], qs.at[h], qr.at[h],
                    device_id=(targets[i], hh), device_id_type=MESH,
                ).start()

            pl.when(j > 0)(functools.partial(ship, 0))
            for i in range(1, GROUP):
                ship(i)

            @pl.when((h == 0) & (j == 0))
            def _():
                @pl.loop(1, N_HEAD)
                def _(k):
                    pltpu.make_async_remote_copy(
                        w_ref, wall.at[:, hh], ws, wr, device_id=(me, (hh + k) % N_HEAD), device_id_type=MESH
                    ).start()

            return shifted(table)

        lax.fori_loop(0, N_SEQ // GROUP, pack, tables())

        @pl.when(h < HEADS - 2)
        def _():
            for copy in loads(h + 2, slot):
                copy.start()

    def arrivals(h):
        others = pl.ds(0, N_SEQ - 1)
        return pltpu.make_async_remote_copy(
            send.at[h, others], recv.at[h, others], qs.at[h], qr.at[h], device_id=(me, hh), device_id_type=MESH
        )

    def returns(h):
        others = pl.ds(0, N_SEQ - 1)
        return pltpu.make_async_remote_copy(
            rsend.at[h, others], rrecv.at[h, others], rs.at[h], rr.at[h], device_id=(me, hh), device_id_type=MESH
        )

    def landing(h, where):
        return y_last.at[:, where] if isinstance(h, int) else ytok.at[h, :, where]

    def exchanged(h):
        return pltpu.make_async_remote_copy(
            atok.at[h, pl.ds(0, N_HEAD - 1)], landing(h, pl.ds(0, (N_HEAD - 1) * HD)), ys.at[h], yr.at[h],
            device_id=(me, hh), device_id_type=MESH,
        )

    @pl.loop(0, HEADS)
    def _(h):
        arrivals(h).wait_recv()

        @pl.loop(0, N_SEQ // GROUP)
        def _(g):
            piece = recv[h, pl.ds(g * GROUP, GROUP)].reshape(ROWS, 3 * HD)
            moved = jnp.dot(perm_ref[...], piece, preferred_element_type=F32).astype(BF)
            for c in range(OWN):
                part = moved[48 * c : 48 * c + 48]
                where = pl.ds(pl.multiple_of(g * 48, 16), 48)
                aq[c, where, :] = part[:, :HD]
                ak[c, where, :] = part[:, HD : 2 * HD]
                av[c, where, :] = part[:, 2 * HD :]

        factor = math.log2(math.e) / math.sqrt(HD)

        def attend(c):
            keys = ak[c]
            values = av[c]
            causal = jnp.where(
                lax.broadcasted_iota(jnp.int32, (BLOCK, BLOCK), 1) <= lax.broadcasted_iota(jnp.int32, (BLOCK, BLOCK), 0),
                0.0, NEG,
            )
            bias = None
            for r in (2, 1, 0):
                width = BLOCK * (r + 1)
                rows = aq[c, BLOCK * r : (MEMBERS + 16 if r == 2 else BLOCK * (r + 1)), :]
                scores = lax.dot_general(
                    rows, keys[:width], (((1,), (1,)), ((), ())), preferred_element_type=F32
                )
                if r == 2:
                    present = jnp.where(scores[BLOCK : BLOCK + 1, :] < MARK / 2, 1.0, 0.0)
                    bias = jnp.where(present > 0.5, 0.0, NEG)
                    present8 = jnp.broadcast_to(present, (8, MEMBERS))
                    sums = jnp.dot(present8.astype(BF), keys, preferred_element_type=F32)[0:1]
                    count = jnp.sum(present, axis=1, keepdims=True)
                    nc_ref[h, pl.ds(c, 1), :] = (PRIOR * cent_ref[h, pl.ds(c, 1), :] + sums) / (PRIOR + count)
                    scores = scores[:BLOCK]
                scores = scores * factor + bias[:, :width]
                last = scores[:, width - BLOCK :] + causal
                scores = last if r == 0 else jnp.concatenate([scores[:, : width - BLOCK], last], axis=1)
                top = jnp.max(scores, axis=1, keepdims=True)
                raw = jnp.exp2(scores - top)
                weights = (raw * (1.0 / jnp.sum(raw, axis=1, keepdims=True))).astype(BF)
                oarr[c, BLOCK * r : BLOCK * r + BLOCK, :] = jnp.dot(
                    weights, values[:width], preferred_element_type=F32
                ).astype(BF)

        pl.loop(0, OWN)(attend)

        @pl.loop(0, N_SEQ // GROUP)
        def _(g):
            piece = oarr[:, pl.ds(pl.multiple_of(g * 48, 16), 48), :].reshape(ROWS, HD)
            moved = jnp.dot(back_ref[...], piece, preferred_element_type=F32).astype(BF)
            rsend[h, pl.ds(g * GROUP, GROUP)] = moved.reshape(GROUP, CHUNK, HD)

        rrecv[h, me] = rsend[h, me]

        def give(j, table):
            targets = four(table)

            def ship(i):
                pltpu.make_async_remote_copy(
                    rsend.at[h, targets[i]], rrecv.at[h, me], rs.at[h], rr.at[h],
                    device_id=(targets[i], hh), device_id_type=MESH,
                ).start()

            pl.when(j > 0)(functools.partial(ship, 0))
            for i in range(1, GROUP):
                ship(i)
            return shifted(table)

        lax.fori_loop(0, N_SEQ // GROUP, give, tables())

    own_weight.wait()
    weights_in = pltpu.make_async_remote_copy(
        wall.at[:, pl.ds(0, N_HEAD - 1)], wall.at[:, pl.ds(0, N_HEAD - 1)], ws, wr,
        device_id=(me, hh), device_id_type=MESH,
    )
    weights_in.wait_recv()
    last_weight = pltpu.make_async_copy(wall.at[HEADS - 1], w_last, os.at[0])
    last_weight.start()

    def project(h):
        exchanged(h).wait_recv()
        for n in range(4):
            cols = slice(512 * n, 512 * n + 512)
            part = jnp.dot(
                ytok[h], wall[h, :, :, cols].reshape(N_HEAD * HD, 512), preferred_element_type=F32
            )
            acc[:, cols] = acc[:, cols] + part

    mine = pl.ds(pl.multiple_of(hh * HD, HD), HD)

    def restore(h):
        returns(h).wait_recv()

        @pl.loop(1, N_HEAD + 1)
        def _(k):
            to = (hh + k) % N_HEAD
            known = lo_ref[h, pl.ds(pl.multiple_of(to * TBLOCK, TBLOCK), TBLOCK), :]
            for j in range(CLUSTERS * CAP // 128):
                pt_ref[:, 128 * j : 128 * j + 128] = one_where(known, BF(j))
            atok[h, to] = jnp.dot(
                pt_ref[...], rrecv[h].reshape(CLUSTERS * CAP, HD), preferred_element_type=F32
            ).astype(BF)

            @pl.when(k < N_HEAD)
            def _():
                pltpu.make_async_remote_copy(
                    atok.at[h, to], landing(h, mine), ys.at[h], yr.at[h], device_id=(me, to), device_id_type=MESH
                ).start()

    acc[...] = jnp.zeros_like(acc)

    @pl.loop(0, HEADS - 1)
    def _(h):
        restore(h)
        ytok[h, :, mine] = atok[h, hh]

        @pl.when(h > 0)
        def _():
            project(h - 1)

    restore(HEADS - 1)
    own_last = pltpu.make_async_copy(atok.at[HEADS - 1, hh], y_last.at[:, mine], os.at[1])
    own_last.start()

    @pl.loop(HEADS - 2, HEADS - 1)
    def _(h):
        project(h)

    total = pltpu.make_async_copy(acc, acc_out, os.at[2])
    total.start()
    exchanged(HEADS - 1).wait_recv()
    own_last.wait()
    last_weight.wait()
    total.wait()

    @pl.loop(0, HEADS)
    def _(h):
        arrivals(h).wait_send()
        returns(h).wait_send()

    @pl.loop(0, HEADS - 1)
    def _(h):
        exchanged(h).wait_send()

    exchanged(HEADS - 1).wait_send()
    weights_in.wait_send()


def finish(acc_ref, y_ref, w_ref, nc_in, out_ref, nc_out):
    out_ref[...] = (acc_ref[...] + jnp.dot(y_ref[...], w_ref[...], preferred_element_type=F32)).astype(BF)
    nc_out[...] = nc_in[...]


def shards(queries, key_rows, value_rows, cluster_ids, centroids, out_weight):
    perm = rearrangement()
    hbm = pl.BlockSpec(memory_space=pl.ANY)
    vmem = pl.BlockSpec(memory_space=pltpu.VMEM)
    total, y_last, w_last, centers = pl.pallas_call(
        kernel,
        out_shape=(
            jax.ShapeDtypeStruct((TBLOCK, 2048), F32),
            jax.ShapeDtypeStruct((TBLOCK, N_HEAD * HD), BF),
            jax.ShapeDtypeStruct((N_HEAD, HD, 2048), BF),
            jax.ShapeDtypeStruct((HEADS, OWN, HD), F32),
        ),
        in_specs=[hbm, hbm, hbm, vmem, vmem, hbm, vmem, vmem],
        out_specs=(hbm, hbm, hbm, vmem),
        scratch_shapes=[
            pltpu.VMEM((2, TOK, 4 * HD), BF),
            pltpu.VMEM((CHUNK, TOK), BF),
            pltpu.VMEM((ROWS, TOK), BF),
            pltpu.VMEM((TBLOCK, CLUSTERS * CAP), BF),
            pltpu.VMEM((HEADS, N_SEQ, CHUNK, 3 * HD), BF),
            pltpu.VMEM((HEADS, N_SEQ, CHUNK, 3 * HD), BF),
            pltpu.VMEM((OWN, MEMBERS + 16, HD), BF),
            pltpu.VMEM((OWN, MEMBERS, HD), BF),
            pltpu.VMEM((OWN, MEMBERS, HD), BF),
            pltpu.VMEM((OWN, MEMBERS, HD), BF),
            pltpu.VMEM((HEADS, N_SEQ, CHUNK, HD), BF),
            pltpu.VMEM((HEADS, N_SEQ, CHUNK, HD), BF),
            pltpu.VMEM((HEADS, TOK, HD), BF),
            pltpu.VMEM((HEADS, N_HEAD, TBLOCK, HD), BF),
            pltpu.VMEM((HEADS - 1, TBLOCK, N_HEAD * HD), BF),
            pltpu.VMEM((HEADS, N_HEAD, HD, 2048), BF),
            pltpu.VMEM((TBLOCK, 2048), F32),
            pltpu.SemaphoreType.DMA((2, 3)),
            pltpu.SemaphoreType.DMA((HEADS,)),
            pltpu.SemaphoreType.DMA((HEADS,)),
            pltpu.SemaphoreType.DMA((HEADS,)),
            pltpu.SemaphoreType.DMA((HEADS,)),
            pltpu.SemaphoreType.DMA((HEADS,)),
            pltpu.SemaphoreType.DMA((HEADS,)),
            pltpu.SemaphoreType.DMA,
            pltpu.SemaphoreType.DMA,
            pltpu.SemaphoreType.DMA,
            pltpu.SemaphoreType.DMA((3,)),
        ],
        compiler_params=pltpu.CompilerParams(
            collective_id=0, has_side_effects=True, vmem_limit_bytes=63 << 20
        ),
    )(
        queries, key_rows, value_rows, cluster_ids.reshape(HEADS * TOK // 128, 128), centroids,
        out_weight.reshape(HEADS, HD, 2048),
        jnp.asarray(perm, BF), jnp.asarray(perm.T, BF),
    )
    tile = 512
    return pl.pallas_call(
        finish,
        grid=(2048 // tile,),
        out_shape=(
            jax.ShapeDtypeStruct((TBLOCK, 2048), BF),
            jax.ShapeDtypeStruct((HEADS, OWN, HD), F32),
        ),
        in_specs=[
            pl.BlockSpec((TBLOCK, tile), lambda n: (0, n)),
            pl.BlockSpec((TBLOCK, N_HEAD * HD), lambda n: (0, 0)),
            pl.BlockSpec((N_HEAD * HD, tile), lambda n: (0, n)),
            pl.BlockSpec((HEADS, OWN, HD), lambda n: (0, 0, 0)),
        ],
        out_specs=(
            pl.BlockSpec((TBLOCK, tile), lambda n: (0, n)),
            pl.BlockSpec((HEADS, OWN, HD), lambda n: (0, 0, 0)),
        ),
    )(total, y_last, w_last.reshape(N_HEAD * HD, 2048), centers)


def solution(mesh):
    placed = (
        P("seq", "head"),
        P("seq", "head"),
        P("seq", "head"),
        P("head", "seq", None),
        P("head", "seq", None),
        P("head", None),
    )
    return jax.shard_map(
        shards,
        mesh=mesh,
        in_specs=placed,
        out_specs=(P(("seq", "head"), None), P("head", "seq", None)),
        check_vma=False,
    )
```

```python
import functools
import math

import jax
import jax.numpy as jnp
import numpy as np
from jax import lax
from jax.experimental import pallas as pl
from jax.experimental.pallas import tpu as pltpu
from jax.sharding import PartitionSpec as P

HD = 128
CLUSTERS = 256
CAP = 12
PRIOR = 8.0
N_SEQ = 32
N_HEAD = 4
OWN = CLUSTERS // N_SEQ
CHUNK = OWN * CAP
TOK = 2048
HEADS = 4
GROUP = 4
ROWS = GROUP * CHUNK
MEMBERS = N_SEQ * CAP
BLOCK = 128
TBLOCK = TOK // N_HEAD
MARK = 64.0
NEG = -1e30
MESH = pl.DeviceIdType.MESH
BF = jnp.bfloat16
F32 = jnp.float32
ORDER = (0, 1, 2, 6, 3, 7, 8, 24, 9, 25, 4, 5, 10, 30, 11, 31, 14, 26, 15, 27, 16, 17, 12, 28, 13, 29, 18, 22, 19, 23, 20, 21)
TABLE = tuple(
    (
        sum(k // 8 * 4**n for n, k in enumerate(ORDER[place::4])),
        sum(k % 8 * 8**n for n, k in enumerate(ORDER[place::4])),
    )
    for place in range(4)
)


def rearrangement():
    src, clu, rank = np.meshgrid(np.arange(GROUP), np.arange(OWN), np.arange(CAP), indexing="ij")
    matrix = np.zeros((ROWS, ROWS), np.float32)
    matrix[(clu * GROUP * CAP + src * CAP + rank).ravel(), (src * CHUNK + clu * CAP + rank).ravel()] = 1
    return matrix


def one_where(held, wanted):
    apart = held - wanted
    return jnp.maximum(BF(1) - apart * apart, BF(0))


def kernel(
    q_ref, k_ref, v_ref, ids_ref, cent_ref, w_ref, perm_ref, back_ref,
    acc_out, y_last, w_last, nc_ref,
    x_ref, base_ref, p_ref, pt_ref, send, recv, aq, ak, av, oarr, rsend, rrecv, lo_ref, atok, ytok, wall, acc,
    xsem, qs, qr, rs, rr, ys, yr, ws, wr, wl, os,
):
    me = lax.axis_index("seq")
    hh = lax.axis_index("head")
    z, x, core = me // 8, (me // 2) % 4, me % 2

    def device_at(dz, dx, dc):
        a = dz + core * (dx - dz)
        b = dx + core * (dz - dx)
        return ((z + a) % 4) * 8 + ((x + b) % 4) * 2 + (core + dc) % 2

    def peer(k):
        return device_at(k // 8, (k // 2) % 4, k % 2)

    def four(table):
        return [device_at(far % 4, (near // 2) % 4, near % 2) for far, near in table]

    def shifted(table):
        return tuple((far // 4, near // 8) for far, near in table)

    def tables():
        return tuple((jnp.int32(far), jnp.int32(near)) for far, near in TABLE)

    def loads(h, slot):
        cols = pl.ds(pl.multiple_of(h * HD, HD), HD)
        return [
            pltpu.make_async_copy(ref.at[:, cols], x_ref.at[slot, :, pl.ds(i * HD, HD)], xsem.at[slot, i])
            for i, ref in enumerate((q_ref, k_ref, v_ref))
        ]

    barrier = pltpu.get_barrier_semaphore()

    @pl.loop(1, N_SEQ)
    def _(k):
        pl.semaphore_signal(barrier, inc=1, device_id=(peer(k), hh), device_id_type=MESH)

    @pl.loop(1, N_HEAD)
    def _(k):
        pl.semaphore_signal(barrier, inc=1, device_id=(me, (hh + k) % N_HEAD), device_id_type=MESH)

    for slot in range(2):
        for copy in loads(slot, slot):
            copy.start()
    own_weight = pltpu.make_async_copy(w_ref, wall.at[:, hh], wl)
    own_weight.start()

    lane0 = lax.broadcasted_iota(jnp.int32, (TOK, HD), 1) == 0
    x_ref[0, :, 3 * HD :] = jnp.where(lane0, MARK, 0.0).astype(BF)
    x_ref[1, :, 3 * HD :] = jnp.where(lane0, MARK, 0.0).astype(BF)
    first = (lax.broadcasted_iota(jnp.int32, (16, HD), 0) == 0) & (lax.broadcasted_iota(jnp.int32, (16, HD), 1) == 0)
    for c in range(OWN):
        aq[c, MEMBERS : MEMBERS + 16, :] = jnp.where(first, 1.0, 0.0).astype(BF)

    @pl.loop(0, HEADS)
    def _(h):
        slot = h % 2
        before = jnp.where(
            lax.broadcasted_iota(jnp.int32, (256, 256), 0) < lax.broadcasted_iota(jnp.int32, (256, 256), 1), 1.0, 0.0
        ).astype(BF)
        cluster = lax.broadcasted_iota(jnp.int32, (CLUSTERS, 256), 0)
        sofar = jnp.zeros((CLUSTERS, 1), F32)
        row96 = lax.broadcasted_iota(jnp.int32, (CHUNK, 256), 0)
        lane = lax.broadcasted_iota(jnp.int32, (256, 128), 1)
        named16 = ids_ref[pl.ds(pl.multiple_of(h * 16, 16), 16), :]
        for b in range(TOK // 256):
            cols = slice(256 * b, 256 * b + 256)
            named = jnp.concatenate([named16[2 * b : 2 * b + 1], named16[2 * b + 1 : 2 * b + 2]], axis=1)
            hot = jnp.where(cluster == named, 1.0, 0.0)
            earlier = jnp.dot(hot.astype(BF), before, preferred_element_type=F32)
            rank = jnp.sum(hot * (earlier + sofar), axis=0, keepdims=True).astype(jnp.int32)
            sofar = sofar + jnp.sum(hot, axis=1, keepdims=True)
            within = (named & 7) * CAP + rank
            owner = (named >> 3).astype(F32)
            base_ref[:, cols] = jnp.where(row96 == within, owner, -1.0).astype(BF)
            place = jnp.broadcast_to((named * CAP + rank).astype(F32), (128, 256)).T.astype(jnp.int32)
            lo_ref[h, cols, :] = jnp.where((place & 127) == lane, (place >> 7).astype(F32), -1.0).astype(BF)
        mark = jnp.where(lax.broadcasted_iota(jnp.int32, (ROWS, HD), 1) == 0, MARK, 0.0)

        for copy in loads(h, slot):
            copy.wait()

        def pack(j, table):
            targets = four(table)
            for i, target in enumerate(targets):
                p_ref[CHUNK * i : CHUNK * i + CHUNK, :] = one_where(base_ref[...], target.astype(F32).astype(BF))
            rows = jnp.dot(p_ref[...], x_ref[slot], preferred_element_type=F32)
            keys = rows[:, HD : 2 * HD] + (mark - rows[:, 3 * HD :])
            rows = jnp.concatenate([rows[:, :HD], keys, rows[:, 2 * HD : 3 * HD]], axis=1).astype(BF)
            rows = rows.reshape(GROUP, CHUNK, 3 * HD)
            send[h, pl.ds(GROUP * j, GROUP)] = rows

            @pl.when(j == 0)
            def _():
                recv[h, me] = rows[0]

            @pl.when((h == 0) & (j == 0))
            def _():
                pl.semaphore_wait(barrier, N_SEQ - 1 + N_HEAD - 1)

            def ship(i):
                pltpu.make_async_remote_copy(
                    send.at[h, GROUP * j + i], recv.at[h, me], qs.at[h], qr.at[h],
                    device_id=(targets[i], hh), device_id_type=MESH,
                ).start()

            pl.when(j > 0)(functools.partial(ship, 0))
            for i in range(1, GROUP):
                ship(i)

            @pl.when((h == 0) & (j == 0))
            def _():
                @pl.loop(1, N_HEAD)
                def _(k):
                    pltpu.make_async_remote_copy(
                        w_ref, wall.at[:, hh], ws, wr, device_id=(me, (hh + k) % N_HEAD), device_id_type=MESH
                    ).start()

            return shifted(table)

        lax.fori_loop(0, N_SEQ // GROUP, pack, tables())

        @pl.when(h < HEADS - 2)
        def _():
            for copy in loads(h + 2, slot):
                copy.start()

    def arrivals(h):
        others = pl.ds(0, N_SEQ - 1)
        return pltpu.make_async_remote_copy(
            send.at[h, others], recv.at[h, others], qs.at[h], qr.at[h], device_id=(me, hh), device_id_type=MESH
        )

    def returns(h):
        others = pl.ds(0, N_SEQ - 1)
        return pltpu.make_async_remote_copy(
            rsend.at[h, others], rrecv.at[h, others], rs.at[h], rr.at[h], device_id=(me, hh), device_id_type=MESH
        )

    def landing(h, where):
        return y_last.at[:, where] if isinstance(h, int) else ytok.at[h, :, where]

    def exchanged(h):
        return pltpu.make_async_remote_copy(
            atok.at[h, pl.ds(0, N_HEAD - 1)], landing(h, pl.ds(0, (N_HEAD - 1) * HD)), ys.at[h], yr.at[h],
            device_id=(me, hh), device_id_type=MESH,
        )

    @pl.loop(0, HEADS)
    def _(h):
        arrivals(h).wait_recv()

        @pl.loop(0, N_SEQ // GROUP)
        def _(g):
            piece = recv[h, pl.ds(g * GROUP, GROUP)].reshape(ROWS, 3 * HD)
            moved = jnp.dot(perm_ref[...], piece, preferred_element_type=F32).astype(BF)
            for c in range(OWN):
                part = moved[48 * c : 48 * c + 48]
                where = pl.ds(pl.multiple_of(g * 48, 16), 48)
                aq[c, where, :] = part[:, :HD]
                ak[c, where, :] = part[:, HD : 2 * HD]
                av[c, where, :] = part[:, 2 * HD :]

        factor = math.log2(math.e) / math.sqrt(HD)

        def attend(c):
            keys = ak[c]
            values = av[c]
            causal = jnp.where(
                lax.broadcasted_iota(jnp.int32, (BLOCK, BLOCK), 1) <= lax.broadcasted_iota(jnp.int32, (BLOCK, BLOCK), 0),
                0.0, NEG,
            )
            bias = None
            for r in (2, 1, 0):
                width = BLOCK * (r + 1)
                rows = aq[c, BLOCK * r : (MEMBERS + 16 if r == 2 else BLOCK * (r + 1)), :]
                scores = lax.dot_general(
                    rows, keys[:width], (((1,), (1,)), ((), ())), preferred_element_type=F32
                )
                if r == 2:
                    present = jnp.where(scores[BLOCK : BLOCK + 1, :] < MARK / 2, 1.0, 0.0)
                    bias = jnp.where(present > 0.5, 0.0, NEG)
                    present8 = jnp.broadcast_to(present, (8, MEMBERS))
                    sums = jnp.dot(present8.astype(BF), keys, preferred_element_type=F32)[0:1]
                    count = jnp.sum(present, axis=1, keepdims=True)
                    nc_ref[h, pl.ds(c, 1), :] = (PRIOR * cent_ref[h, pl.ds(c, 1), :] + sums) / (PRIOR + count)
                    scores = scores[:BLOCK]
                scores = scores * factor + bias[:, :width]
                last = scores[:, width - BLOCK :] + causal
                scores = last if r == 0 else jnp.concatenate([scores[:, : width - BLOCK], last], axis=1)
                top = jnp.max(scores, axis=1, keepdims=True)
                raw = jnp.exp2(scores - top)
                weights = (raw * (1.0 / jnp.sum(raw, axis=1, keepdims=True))).astype(BF)
                oarr[c, BLOCK * r : BLOCK * r + BLOCK, :] = jnp.dot(
                    weights, values[:width], preferred_element_type=F32
                ).astype(BF)

        pl.loop(0, OWN)(attend)

        @pl.loop(0, N_SEQ // GROUP)
        def _(g):
            piece = oarr[:, pl.ds(pl.multiple_of(g * 48, 16), 48), :].reshape(ROWS, HD)
            moved = jnp.dot(back_ref[...], piece, preferred_element_type=F32).astype(BF)
            rsend[h, pl.ds(g * GROUP, GROUP)] = moved.reshape(GROUP, CHUNK, HD)

        rrecv[h, me] = rsend[h, me]

        def give(j, table):
            targets = four(table)

            def ship(i):
                pltpu.make_async_remote_copy(
                    rsend.at[h, targets[i]], rrecv.at[h, me], rs.at[h], rr.at[h],
                    device_id=(targets[i], hh), device_id_type=MESH,
                ).start()

            pl.when(j > 0)(functools.partial(ship, 0))
            for i in range(1, GROUP):
                ship(i)
            return shifted(table)

        lax.fori_loop(0, N_SEQ // GROUP, give, tables())

    own_weight.wait()
    weights_in = pltpu.make_async_remote_copy(
        wall.at[:, pl.ds(0, N_HEAD - 1)], wall.at[:, pl.ds(0, N_HEAD - 1)], ws, wr,
        device_id=(me, hh), device_id_type=MESH,
    )
    weights_in.wait_recv()
    last_weight = pltpu.make_async_copy(wall.at[HEADS - 1], w_last, os.at[0])
    last_weight.start()

    def project(h):
        exchanged(h).wait_recv()
        for n in range(4):
            cols = slice(512 * n, 512 * n + 512)
            part = jnp.dot(
                ytok[h], wall[h, :, :, cols].reshape(N_HEAD * HD, 512), preferred_element_type=F32
            )
            acc[:, cols] = acc[:, cols] + part

    mine = pl.ds(pl.multiple_of(hh * HD, HD), HD)

    def restore(h):
        returns(h).wait_recv()

        @pl.loop(1, N_HEAD + 1)
        def _(n):
            late = n // 3
            k = late * n + (1 - late) * (3 - n)
            to = (hh + k) % N_HEAD
            known = lo_ref[h, pl.ds(pl.multiple_of(to * TBLOCK, TBLOCK), TBLOCK), :]
            for j in range(CLUSTERS * CAP // 128):
                pt_ref[:, 128 * j : 128 * j + 128] = one_where(known, BF(j))
            atok[h, to] = jnp.dot(
                pt_ref[...], rrecv[h].reshape(CLUSTERS * CAP, HD), preferred_element_type=F32
            ).astype(BF)

            @pl.when(k < N_HEAD)
            def _():
                pltpu.make_async_remote_copy(
                    atok.at[h, to], landing(h, mine), ys.at[h], yr.at[h], device_id=(me, to), device_id_type=MESH
                ).start()

    acc[...] = jnp.zeros_like(acc)

    @pl.loop(0, HEADS - 1)
    def _(h):
        restore(h)
        ytok[h, :, mine] = atok[h, hh]

        @pl.when(h > 0)
        def _():
            project(h - 1)

    restore(HEADS - 1)
    own_last = pltpu.make_async_copy(atok.at[HEADS - 1, hh], y_last.at[:, mine], os.at[1])
    own_last.start()

    @pl.loop(HEADS - 2, HEADS - 1)
    def _(h):
        project(h)

    total = pltpu.make_async_copy(acc, acc_out, os.at[2])
    total.start()
    exchanged(HEADS - 1).wait_recv()
    own_last.wait()
    last_weight.wait()
    total.wait()

    @pl.loop(0, HEADS)
    def _(h):
        arrivals(h).wait_send()
        returns(h).wait_send()

    @pl.loop(0, HEADS - 1)
    def _(h):
        exchanged(h).wait_send()

    exchanged(HEADS - 1).wait_send()
    weights_in.wait_send()


def finish(acc_ref, y_ref, w_ref, nc_in, out_ref, nc_out):
    out_ref[...] = (acc_ref[...] + jnp.dot(y_ref[...], w_ref[...], preferred_element_type=F32)).astype(BF)
    nc_out[...] = nc_in[...]


def shards(queries, key_rows, value_rows, cluster_ids, centroids, out_weight):
    perm = rearrangement()
    hbm = pl.BlockSpec(memory_space=pl.ANY)
    vmem = pl.BlockSpec(memory_space=pltpu.VMEM)
    total, y_last, w_last, centers = pl.pallas_call(
        kernel,
        out_shape=(
            jax.ShapeDtypeStruct((TBLOCK, 2048), F32),
            jax.ShapeDtypeStruct((TBLOCK, N_HEAD * HD), BF),
            jax.ShapeDtypeStruct((N_HEAD, HD, 2048), BF),
            jax.ShapeDtypeStruct((HEADS, OWN, HD), F32),
        ),
        in_specs=[hbm, hbm, hbm, vmem, vmem, hbm, vmem, vmem],
        out_specs=(hbm, hbm, hbm, vmem),
        scratch_shapes=[
            pltpu.VMEM((2, TOK, 4 * HD), BF),
            pltpu.VMEM((CHUNK, TOK), BF),
            pltpu.VMEM((ROWS, TOK), BF),
            pltpu.VMEM((TBLOCK, CLUSTERS * CAP), BF),
            pltpu.VMEM((HEADS, N_SEQ, CHUNK, 3 * HD), BF),
            pltpu.VMEM((HEADS, N_SEQ, CHUNK, 3 * HD), BF),
            pltpu.VMEM((OWN, MEMBERS + 16, HD), BF),
            pltpu.VMEM((OWN, MEMBERS, HD), BF),
            pltpu.VMEM((OWN, MEMBERS, HD), BF),
            pltpu.VMEM((OWN, MEMBERS, HD), BF),
            pltpu.VMEM((HEADS, N_SEQ, CHUNK, HD), BF),
            pltpu.VMEM((HEADS, N_SEQ, CHUNK, HD), BF),
            pltpu.VMEM((HEADS, TOK, HD), BF),
            pltpu.VMEM((HEADS, N_HEAD, TBLOCK, HD), BF),
            pltpu.VMEM((HEADS - 1, TBLOCK, N_HEAD * HD), BF),
            pltpu.VMEM((HEADS, N_HEAD, HD, 2048), BF),
            pltpu.VMEM((TBLOCK, 2048), F32),
            pltpu.SemaphoreType.DMA((2, 3)),
            pltpu.SemaphoreType.DMA((HEADS,)),
            pltpu.SemaphoreType.DMA((HEADS,)),
            pltpu.SemaphoreType.DMA((HEADS,)),
            pltpu.SemaphoreType.DMA((HEADS,)),
            pltpu.SemaphoreType.DMA((HEADS,)),
            pltpu.SemaphoreType.DMA((HEADS,)),
            pltpu.SemaphoreType.DMA,
            pltpu.SemaphoreType.DMA,
            pltpu.SemaphoreType.DMA,
            pltpu.SemaphoreType.DMA((3,)),
        ],
        compiler_params=pltpu.CompilerParams(
            collective_id=0, has_side_effects=True, vmem_limit_bytes=63 << 20
        ),
    )(
        queries, key_rows, value_rows, cluster_ids.reshape(HEADS * TOK // 128, 128), centroids,
        out_weight.reshape(HEADS, HD, 2048),
        jnp.asarray(perm, BF), jnp.asarray(perm.T, BF),
    )
    tile = 1024
    return pl.pallas_call(
        finish,
        grid=(2048 // tile,),
        out_shape=(
            jax.ShapeDtypeStruct((TBLOCK, 2048), BF),
            jax.ShapeDtypeStruct((HEADS, OWN, HD), F32),
        ),
        in_specs=[
            pl.BlockSpec((TBLOCK, tile), lambda n: (0, n)),
            pl.BlockSpec((TBLOCK, N_HEAD * HD), lambda n: (0, 0)),
            pl.BlockSpec((N_HEAD * HD, tile), lambda n: (0, n)),
            pl.BlockSpec((HEADS, OWN, HD), lambda n: (0, 0, 0)),
        ],
        out_specs=(
            pl.BlockSpec((TBLOCK, tile), lambda n: (0, n)),
            pl.BlockSpec((HEADS, OWN, HD), lambda n: (0, 0, 0)),
        ),
    )(total, y_last, w_last.reshape(N_HEAD * HD, 2048), centers)


def solution(mesh):
    placed = (
        P("seq", "head"),
        P("seq", "head"),
        P("seq", "head"),
        P("head", "seq", None),
        P("head", "seq", None),
        P("head", None),
    )
    return jax.shard_map(
        shards,
        mesh=mesh,
        in_specs=placed,
        out_specs=(P(("seq", "head"), None), P("head", "seq", None)),
        check_vma=False,
    )
```
